32 devices in a mesh: groups: 2 (over x), row: 16 (over z, y, core).
Axes of the slice: x: 2, y: 2, z: 4, core: 2. Of those that a mesh axis runs over, the one named last changes fastest.
Arguments:
- pair_act: bfloat16 [3072, 256, 128], P(('groups', 'row')), parts along dimension 0, may hold values from -36 to 36
- pair_mask: int32 [3072, 256], P(('groups', 'row')), parts along dimension 0, may hold values from 0 to 1, as said below
- in_gain: float32 [128], replicated, may hold values from 0.25 to 1.75
- in_bias: float32 [128], replicated, may hold values from -3 to 3
- w_proj: bfloat16 [128, 256], replicated, may hold values from -0.5 to 0.5
- w_gate: bfloat16 [128, 128], replicated, may hold values from -0.5 to 0.5
- out_gain: float32 [64], replicated, may hold values from 0.25 to 1.75
- out_bias: float32 [64], replicated, may hold values from -3 to 3
- w_out: bfloat16 [64, 128], replicated, may hold values from -0.75 to 0.75
Outputs:
- update: bfloat16 [512, 256, 128], P(('groups', 'row')), parts along dimension 0
The draws below stay inside these ranges and needn't reach their ends.
There are 2 independent parts, one for each index of `groups`. The reference program is written for one: setup_inputs(seed, part) draws one part's arguments, and reference() takes and returns one part's arrays. A program takes and returns all parts, laid end to end along the dimension named above; an argument that names none is the same for every part. Nothing has to cross between parts.
Inputs may be any that keep to these rules, and one draw needn't show every extreme that they name: pair_mask[k, w] is 1 exactly where both token k and the token of window token w are below the complex's length, which is 768 or more, else 0.
All inputs are finite; a program needn't handle non-finite values.
Results may differ from the reference program's by a relative error of at most 0.0053.
Values may be sent and summed in bfloat16 or wider, within the bound.
No kernel may reach another device: no remote copies, remote signals or barrier semaphores. Data moves between devices by JAX's collectives and lax.ppermute only.
A program may use at most 320 MiB of HBM per device.

```python
import math
import jax
import jax.numpy as jnp
from jax import lax

C = 128
H = 64
ROWS_DEV = 96
OUT_DEV = 16
N = 1536
W = 256


def draw_pair_act(key, part):
    key = jax.random.fold_in(key, 11)
    key_base, key_pair, key_chan = jax.random.split(key, 3)
    pair_scale = jnp.exp(jax.random.uniform(key_pair, (N, W, 1), jnp.float32, math.log(0.3), math.log(3.0)))
    chan_scale = jnp.exp(jax.random.uniform(key_chan, (C,), jnp.float32, math.log(0.3), math.log(3.0)))
    base_vals = jax.random.normal(key_base, (N, W, C), jnp.float32)
    base_vals = jnp.clip(base_vals, -4.0, 4.0)
    return (base_vals * pair_scale * chan_scale).astype(jnp.bfloat16)


def draw_pair_mask(key, part):
    key = jax.random.fold_in(key, 23)
    length = jax.random.randint(key, (), N // 2, N + 1)
    token_rows = jnp.arange(N, dtype=jnp.int32)
    window_idx = jnp.arange(W, dtype=jnp.int32)
    token_cols = window_idx // OUT_DEV * ROWS_DEV + window_idx % OUT_DEV
    valid_rows = token_rows < length
    valid_cols = token_cols < length
    return (valid_rows[:, None] & valid_cols[None, :]).astype(jnp.int32)


def scatter_about(own_key, extent, width, most, held_as=jnp.bfloat16):
    entries = jax.random.normal(own_key, extent, jnp.float32) * width
    return jnp.minimum(jnp.maximum(entries, -most), most).astype(held_as)


def setup_inputs(seed: int = 0, part: int = 0) -> dict:
    keys = jax.random.split(jax.random.key(seed), 10)
    part_splits = jax.random.split(jax.random.fold_in(keys[9], part), 10)
    pair_act = draw_pair_act(jax.random.fold_in(jax.random.fold_in(keys[9], part), 71), part)
    pair_mask = draw_pair_mask(jax.random.fold_in(jax.random.fold_in(keys[9], part), 71), part)
    in_gain = jnp.clip(1.0 + 0.15 * jax.random.normal(keys[2], (C,), jnp.float32), 0.25, 1.75)
    in_bias = scatter_about(keys[3], (C,), 0.5, 3.0, jnp.float32)
    w_proj = scatter_about(keys[4], (C, 4 * H), C ** -0.5, 0.5)
    w_gate = scatter_about(keys[5], (C, C), C ** -0.5, 0.5)
    out_gain = jnp.clip(1.0 + 0.15 * jax.random.normal(keys[6], (H,), jnp.float32), 0.25, 1.75)
    out_bias = scatter_about(keys[7], (H,), 0.5, 3.0, jnp.float32)
    w_out = scatter_about(keys[8], (H, C), H ** -0.5, 0.75)
    return dict(pair_act=pair_act, pair_mask=pair_mask, in_gain=in_gain, in_bias=in_bias, w_proj=w_proj, w_gate=w_gate, out_gain=out_gain, out_bias=out_bias, w_out=w_out)


def normalize(values, gain_vec, bias_vec, reduce_axis):
    mean_val = lax.optimization_barrier(jnp.mean(values, axis=reduce_axis, keepdims=True))
    centered = values - mean_val
    variance = lax.optimization_barrier(jnp.mean(centered * centered, axis=reduce_axis, keepdims=True))
    return centered * lax.rsqrt(variance + 1e-05) * gain_vec + bias_vec

def reference(pair_act, pair_mask, in_gain, in_bias, w_proj, w_gate, out_gain, out_bias, w_out):
    normed = normalize(pair_act.astype(jnp.float32), in_gain, in_bias, -1).astype(jnp.bfloat16)
    flat_normed = normed.reshape(N * W, C)
    projected = jnp.dot(flat_normed, w_proj, preferred_element_type=jnp.float32).reshape(N, W, 4 * H)
    keep_mask = pair_mask.astype(jnp.float32)[:, :, None]
    left_act = (jax.nn.sigmoid(projected[:, :, :H]) * projected[:, :, H:2 * H] * keep_mask).astype(jnp.bfloat16)
    right_act = (jax.nn.sigmoid(projected[:, :, 2 * H:3 * H]) * projected[:, :, 3 * H:] * keep_mask).astype(jnp.bfloat16)
    triangle = jnp.einsum('kih,kjh->ijh', left_act.astype(jnp.float32), right_act.astype(jnp.float32), precision=lax.Precision.HIGHEST)
    triangle_norm = normalize(triangle, out_gain, out_bias, -1).astype(jnp.bfloat16)
    window_idx = jnp.arange(W, dtype=jnp.int32)
    token_idx = (window_idx // OUT_DEV * ROWS_DEV + window_idx % OUT_DEV).astype(jnp.int32)
    window_normed = jnp.take(normed, token_idx, axis=0).reshape(W * W, C)
    gate_act = jax.nn.sigmoid(jnp.dot(window_normed, w_gate, preferred_element_type=jnp.float32))
    mixed = jnp.dot(triangle_norm.reshape(W * W, H), w_out, preferred_element_type=jnp.float32)
    return (gate_act * mixed).reshape(W, W, C).astype(jnp.bfloat16)
```

```python
import functools

import jax
import jax.numpy as jnp
from jax import lax
from jax.experimental import pallas as pl
from jax.experimental.pallas import tpu as pltpu
from jax.sharding import PartitionSpec as P

f32 = jnp.float32
bf16 = jnp.bfloat16
LANES = 128
EPS = 1e-05
VMEM_BYTES = 40 * 2**20


def sigmoid(values):
    return 0.5 * jnp.tanh(0.5 * values) + 0.5


def whole(shape):
    return pl.BlockSpec(shape, lambda *_: (0,) * len(shape))


def call(body, grid, in_specs, out_specs, out_shape, scratch, cost, prefetch=1):
    return pl.pallas_call(
        body,
        grid_spec=pltpu.PrefetchScalarGridSpec(
            num_scalar_prefetch=prefetch,
            grid=grid,
            in_specs=in_specs,
            out_specs=out_specs,
            scratch_shapes=scratch,
        ),
        out_shape=out_shape,
        compiler_params=pltpu.CompilerParams(vmem_limit_bytes=VMEM_BYTES),
        cost_estimate=pl.CostEstimate(flops=cost[0], bytes_accessed=cost[1], transcendentals=0),
    )


def norm_columns(tile, gain, bias):
    count = tile.shape[0]
    mean_val = jnp.sum(tile, axis=0, keepdims=True) * (1.0 / count)
    centered = tile - mean_val
    variance = jnp.sum(centered * centered, axis=0, keepdims=True) * (1.0 / count)
    return (centered * lax.rsqrt(variance + EPS) * gain + bias).astype(bf16)


def spread(vec_ref, width):
    tile = jnp.broadcast_to(vec_ref[...], (vec_ref.shape[0], LANES))
    return jnp.concatenate([tile] * (width // LANES), axis=1)


def project_body(chunks, stride, place, x_ref, mask_ref, gain_ref, bias_ref, w_ref, *rest):
    count = len(chunks)
    outs, hold = (rest[:count], rest[count : 2 * count]), rest[2 * count]
    rows, width, _ = x_ref.shape
    hidden = w_ref.shape[1] // 4
    half = hidden // 2
    gain, bias = spread(gain_ref, width), spread(bias_ref, width)
    weights = w_ref[...]
    for k in range(rows):
        normed = norm_columns(x_ref[k].T.astype(f32), gain, bias)
        proj = lax.dot_general(weights, normed, (((0,), (0,)), ((), ())), preferred_element_type=f32)
        keep = mask_ref[pl.ds(k, 1), :].astype(f32)
        for side in range(2):
            low = 2 * side * hidden
            act = sigmoid(proj[low : low + hidden]) * proj[low + hidden : low + 2 * hidden] * keep
            for part in range(width // LANES):
                hold[part, pl.ds(k * stride + side * hidden, hidden), :] = act[
                    :, part * LANES : (part + 1) * LANES
                ]
    core = place[2]
    for owner in range(2):
        base = jnp.where(core == owner, 0, half)
        first = 0
        for out, size in zip(outs[owner], chunks):
            for side in range(2):
                for h in range(size):
                    for part in range(width // LANES):
                        tile = hold[part, pl.ds(base + side * hidden + first + h, rows, stride=stride), :]
                        out[side, h, :, part * LANES : (part + 1) * LANES] = tile.astype(bf16)
            first += size


def project(place, x, mask, gain, bias, w_proj, chunks):
    depth, width, chan = x.shape
    rows = 16
    hidden = w_proj.shape[1] // 4
    stride = 2 * hidden + 8
    return call(
        functools.partial(project_body, chunks, stride),
        (depth // rows,),
        [
            pl.BlockSpec((rows, width, chan), lambda i, _: (i, 0, 0)),
            pl.BlockSpec((rows, width), lambda i, _: (i, 0)),
            whole((chan, 1)),
            whole((chan, 1)),
            whole(w_proj.shape),
        ],
        [pl.BlockSpec((2, size, rows, width), lambda i, _: (0, 0, i, 0)) for size in chunks] * 2,
        [jax.ShapeDtypeStruct((2, size, depth, width), bf16) for size in chunks] * 2,
        [pltpu.VMEM((width // LANES, rows * stride, LANES), f32)],
        (2 * depth * width * chan * 4 * hidden, 4 * depth * width * chan),
    )(place, x, mask, gain.reshape(chan, 1), bias.reshape(chan, 1), w_proj)


def gate_body(x_ref, gain_ref, bias_ref, w_ref, out_ref):
    width = x_ref.shape[1]
    gain, bias = spread(gain_ref, width), spread(bias_ref, width)
    weights = w_ref[...]
    for k in range(x_ref.shape[0]):
        normed = norm_columns(x_ref[k].T.astype(f32), gain, bias)
        proj = lax.dot_general(normed, weights, (((0,), (0,)), ((), ())), preferred_element_type=f32)
        out_ref[k] = sigmoid(proj)


def gate(x, gain, bias, w_gate, rows):
    _, width, chan = x.shape
    step = 8
    return call(
        gate_body,
        (rows // step,),
        [
            pl.BlockSpec((step, width, chan), lambda i: (i, 0, 0)),
            whole((chan, 1)),
            whole((chan, 1)),
            whole(w_gate.shape),
        ],
        pl.BlockSpec((step, width, chan), lambda i: (i, 0, 0)),
        jax.ShapeDtypeStruct((rows, width, chan), f32),
        [],
        (2 * rows * width * chan * chan, 6 * rows * width * chan),
        prefetch=0,
    )(x, gain.reshape(chan, 1), bias.reshape(chan, 1), w_gate)


def triangle_body(place, own_ref, got_ref, keep_ref, send_ref, hold):
    _, step, layers, block, width = (0,) + keep_ref.shape
    layer, column = place[0], place[1]
    for h in range(step):
        left = jnp.concatenate([own_ref[0, h], got_ref[0, h]], axis=0)
        right = jnp.concatenate([own_ref[1, h], got_ref[1, h]], axis=0)
        hold[h] = lax.dot_general(left, right, (((0,), (0,)), ((), ())), preferred_element_type=f32)
        for slot in range(layers):
            first = ((layer ^ slot) * 2 + column) * block
            other = ((layer ^ slot) * 2 + 1 - column) * block
            keep_ref[h, slot] = hold[h, pl.ds(pl.multiple_of(first, block), block), :]
            send_ref[h, slot] = hold[h, pl.ds(pl.multiple_of(other, block), block), :].astype(bf16)


def triangle(place, own, got, layers):
    _, size, depth, width = own.shape
    step = min(size, 4)
    block = width // (2 * layers)
    spec = pl.BlockSpec((2, step, depth, width), lambda i, _: (0, i, 0, 0))
    out_spec = pl.BlockSpec((step, layers, block, width), lambda i, _: (i, 0, 0, 0))
    shape = (size, layers, block, width)
    return call(
        triangle_body,
        (size // step,),
        [spec, spec],
        [out_spec, out_spec],
        [jax.ShapeDtypeStruct(shape, f32), jax.ShapeDtypeStruct(shape, bf16)],
        [pltpu.VMEM((step, width, width), f32)],
        (4 * size * depth * width * width, 8 * size * depth * width + 3 * size * width * width),
    )(place, own, got)


def layer_body(keep_ref, got_ref, own_ref, *send_refs):
    own_ref[...] = keep_ref[:, 0] + got_ref[:, 0].astype(f32)
    for slot, send_ref in enumerate(send_refs, 1):
        send_ref[...] = (keep_ref[:, slot] + got_ref[:, slot].astype(f32)).astype(bf16)


def layer_sum(keep, got):
    size, layers, block, width = keep.shape
    step = min(size, 4)
    spec = pl.BlockSpec((step, layers, block, width), lambda i: (i, 0, 0, 0))
    out_spec = pl.BlockSpec((step, block, width), lambda i: (i, 0, 0))
    shape = (size, block, width)
    return call(
        layer_body,
        (size // step,),
        [spec, spec],
        [out_spec] * layers,
        [jax.ShapeDtypeStruct(shape, f32)] + [jax.ShapeDtypeStruct(shape, bf16)] * (layers - 1),
        [],
        (keep.size, keep.size * 8),
        prefetch=0,
    )(keep, got)


def total_body(place, own_ref, *rest):
    got_refs, (mine_ref, theirs_ref, hold) = rest[:-3], rest[-3:]
    total = own_ref[...]
    for got_ref in got_refs:
        total = total + got_ref[...].astype(f32)
    hold[...] = total
    rows = mine_ref.shape[1]
    core = place[2]
    mine_ref[...] = hold[:, pl.ds(pl.multiple_of(core * rows, rows), rows), :]
    theirs_ref[...] = hold[:, pl.ds(pl.multiple_of((1 - core) * rows, rows), rows), :]


def total_sum(place, own, gots):
    size, block, width = own.shape
    step = min(size, 4)
    spec = pl.BlockSpec((step, block, width), lambda i, _: (i, 0, 0))
    out_spec = pl.BlockSpec((step, block // 2, width), lambda i, _: (i, 0, 0))
    shape = jax.ShapeDtypeStruct((size, block // 2, width), f32)
    return call(
        total_body,
        (size // step,),
        [spec] * (1 + len(gots)),
        [out_spec] * 2,
        [shape, shape],
        [pltpu.VMEM((step, block, width), f32)],
        (own.size * len(gots), own.size * (8 + 2 * len(gots))),
    )(place, own, *gots)


def finish_body(chunks, place, *refs):
    count = len(chunks)
    mine, theirs = refs[:count], refs[count : 2 * count]
    gate_ref, gain_ref, bias_ref, w_ref, out_ref, hold = refs[2 * count :]
    hidden, _ = w_ref.shape
    half = hidden // 2
    _, rows, width = mine[0].shape
    stride = hold.shape[1] // hidden
    core = place[2]
    total = jnp.zeros((rows, width), f32)
    for part in mine + theirs:
        total = total + jnp.sum(part[...], axis=0)
    mean_val = total * (1.0 / hidden)
    square = jnp.zeros((rows, width), f32)
    for part in mine + theirs:
        for h in range(part.shape[0]):
            centered = part[h] - mean_val
            square = square + centered * centered
    scale = lax.rsqrt(square * (1.0 / hidden) + EPS)
    for owner, parts in ((0, mine), (1, theirs)):
        index = jnp.where(core == owner, 0, half)
        for part in parts:
            for h in range(part.shape[0]):
                value = (part[h] - mean_val) * scale * gain_ref[index] + bias_ref[index]
                for lane in range(width // LANES):
                    hold[lane, pl.ds(index * stride, rows), :] = value[:, lane * LANES : (lane + 1) * LANES]
                index = index + 1
    weights = w_ref[...]
    for row in range(rows):
        for lane in range(width // LANES):
            normed = hold[lane, pl.ds(row, hidden, stride=stride), :].astype(bf16)
            mixed = lax.dot_general(normed, weights, (((0,), (0,)), ((), ())), preferred_element_type=f32)
            span = pl.ds(lane * LANES, LANES)
            out_ref[row, span, :] = (gate_ref[row, span, :] * mixed).astype(bf16)


def finish(place, mine, theirs, gate_act, gain, bias, w_out):
    rows, width, chan = gate_act.shape
    hidden = w_out.shape[0]
    step = 8
    stride = step + 8
    parts = [pl.BlockSpec((part.shape[0], step, width), lambda i, _: (0, i, 0)) for part in mine]
    spec = pl.BlockSpec((step, width, chan), lambda i, _: (i, 0, 0))
    smem = pl.BlockSpec(memory_space=pltpu.SMEM)
    return call(
        functools.partial(finish_body, [part.shape[0] for part in mine]),
        (rows // step,),
        parts * 2 + [spec, smem, smem, whole(w_out.shape)],
        spec,
        jax.ShapeDtypeStruct((rows, width, chan), bf16),
        [pltpu.VMEM((width // LANES, hidden * stride, LANES), f32)],
        (2 * rows * width * chan * hidden, rows * width * (chan * 6 + hidden * 4)),
    )(place, *mine, *theirs, gate_act, gain, bias, w_out)


def on_device(pair_act, pair_mask, in_gain, in_bias, w_proj, w_gate, out_gain, out_bias, w_out):
    width = pair_act.shape[1]
    devices = lax.axis_size("row")
    layers = devices // 4
    half = w_out.shape[0] // 2
    chunks = (half // 4,) * 4
    index = lax.axis_index("row")
    place = jnp.stack([index // 4, index // 2 % 2, index % 2]).astype(jnp.int32)

    def swap(values, bit):
        return lax.ppermute(values, "row", [(d, d ^ bit) for d in range(devices)])

    acts = project(place, pair_act, pair_mask, in_gain, in_bias, w_proj, chunks)
    count = len(chunks)
    got = [swap(part, 1) for part in acts[count:]]
    gate_act = gate(pair_act, in_gain, in_bias, w_gate, width // devices)
    mine, theirs = [], []
    for own, other in zip(acts[:count], got):
        keep, send = triangle(place, own, other, layers)
        own_sum, *sends = layer_sum(keep, swap(send, 2))
        gots = [swap(part, 4 * slot) for slot, part in enumerate(sends, 1)]
        mine_part, send_part = total_sum(place, own_sum, gots)
        mine.append(mine_part)
        theirs.append(swap(send_part, 1))
    return finish(place, mine, theirs, gate_act, out_gain, out_bias, w_out)


def solution(mesh):
    return jax.shard_map(
        on_device,
        mesh=mesh,
        in_specs=(
            P(("groups", "row"), None, None),
            P(("groups", "row"), None),
            P(),
            P(),
            P(),
            P(),
            P(),
            P(),
            P(),
        ),
        out_specs=P(("groups", "row"), None, None),
        check_vma=False,
    )
```

```python
import functools

import jax
import jax.numpy as jnp
from jax import lax
from jax.experimental import pallas as pl
from jax.experimental.pallas import tpu as pltpu
from jax.sharding import PartitionSpec as P

f32 = jnp.float32
bf16 = jnp.bfloat16
LANES = 128
EPS = 1e-05
VMEM_BYTES = 12 * 2**20
PROJECT_ROWS = 16


def whole(shape):
    return pl.BlockSpec(shape, lambda *_: (0,) * len(shape))


def call(body, grid, in_specs, out_specs, out_shape, scratch, cost, operands, after=(), vmem=VMEM_BYTES):
    count = len(operands)
    extra = len(after)

    def run(*refs):
        return body(*refs[:count], *refs[count + extra :])

    return pl.pallas_call(
        run,
        grid_spec=pltpu.PrefetchScalarGridSpec(
            num_scalar_prefetch=1,
            grid=grid,
            in_specs=list(in_specs) + [pl.BlockSpec(memory_space=pl.ANY)] * extra,
            out_specs=out_specs,
            scratch_shapes=scratch,
        ),
        out_shape=out_shape,
        compiler_params=pltpu.CompilerParams(vmem_limit_bytes=vmem),
        cost_estimate=pl.CostEstimate(flops=cost[0], bytes_accessed=cost[1], transcendentals=0),
    )(*operands, *after)


def norm_columns(tile, gain, bias):
    count = tile.shape[0]
    mean_val = jnp.sum(tile, axis=0, keepdims=True) * (1.0 / count)
    centered = tile - mean_val
    variance = jnp.sum(centered * centered, axis=0, keepdims=True) * (1.0 / count)
    return (centered * lax.rsqrt(variance + EPS) * gain + bias).astype(bf16)


def gather_weights(w_ref, wt_ref, first, size):
    hidden = w_ref.shape[1] // 4
    half = hidden // 2
    turned = w_ref[...].astype(f32).T * 0.5
    row = 0
    for value in range(2):
        for side in range(2):
            for part in range(2):
                low = (2 * side + value) * hidden + part * half + first
                wt_ref[row : row + size, :] = turned[low : low + size]
                row += size


def turn_affine(gain_ref, bias_ref, affine_ref):
    chan = gain_ref.shape[1]
    affine_ref[0] = jnp.broadcast_to(gain_ref[...], (LANES, chan)).T
    affine_ref[1] = jnp.broadcast_to(bias_ref[...], (LANES, chan)).T


def normed_row(x_ref, affine_ref, k):
    parts = [
        norm_columns(x_ref[k, low : low + LANES, :].T.astype(f32), affine_ref[0], affine_ref[1])
        for low in range(0, x_ref.shape[1], LANES)
    ]
    return jnp.concatenate(parts, axis=1)


def project_body(chunks, first, stride, place, x_ref, mask_ref, gain_ref, bias_ref, w_ref, *rest):
    count = len(chunks)
    outs, (hold, wt_ref, affine_ref) = (rest[:count], rest[count : 2 * count]), rest[2 * count :]
    rows, width, _ = x_ref.shape
    size = sum(chunks)

    @pl.when(pl.program_id(0) == 0)
    def _():
        gather_weights(w_ref, wt_ref, first, size)
        turn_affine(gain_ref, bias_ref, affine_ref)

    weights = wt_ref[...].astype(bf16)
    for k in range(rows):
        proj = jnp.dot(weights, normed_row(x_ref, affine_ref, k), preferred_element_type=f32)
        keep = mask_ref[pl.ds(k, 1), :].astype(f32)
        act = (jnp.tanh(proj[: 4 * size]) + 1.0) * proj[4 * size :] * keep
        for lane in range(width // LANES):
            hold[lane, pl.ds(k * stride, 4 * size), :] = act[:, lane * LANES : (lane + 1) * LANES]
    for owner in range(2):
        base = jnp.where(place[2] == owner, 0, size)
        offset = 0
        for out, count in zip(outs[owner], chunks):
            for side in range(2):
                for h in range(count):
                    for lane in range(width // LANES):
                        start = base + 2 * side * size + offset + h
                        tile = hold[lane, pl.ds(start, rows, stride=stride), :]
                        out[side, h, :, lane * LANES : (lane + 1) * LANES] = tile.astype(bf16)
            offset += count


def project(place, x, mask, gain, bias, w_proj, chunks, first, vmem, after):
    depth, width, chan = x.shape
    rows, size = PROJECT_ROWS, sum(chunks)
    stride = 4 * size + 8
    return call(
        functools.partial(project_body, chunks, first, stride),
        (depth // rows,),
        [
            pl.BlockSpec((rows, width, chan), lambda i, _: (i, 0, 0)),
            pl.BlockSpec((rows, width), lambda i, _: (i, 0)),
            whole((1, chan)),
            whole((1, chan)),
            whole(w_proj.shape),
        ],
        [pl.BlockSpec((2, size, rows, width), lambda i, _: (0, 0, i, 0)) for size in chunks] * 2,
        [jax.ShapeDtypeStruct((2, size, depth, width), bf16) for size in chunks] * 2,
        [
            pltpu.VMEM((width // LANES, rows * stride, LANES), f32),
            pltpu.VMEM((8 * size, chan), f32),
            pltpu.VMEM((2, chan, LANES), f32),
        ],
        (2 * depth * width * chan * 8 * size, 4 * depth * width * chan),
        (place, x, mask, gain.reshape(1, chan), bias.reshape(1, chan), w_proj),
        after,
        vmem,
    )


def gate_body(place, x_ref, gain_ref, bias_ref, w_ref, out_ref, affine_ref):
    @pl.when(pl.program_id(0) == 0)
    def _():
        turn_affine(gain_ref, bias_ref, affine_ref)

    weights = w_ref[...]
    for k in range(x_ref.shape[0]):
        normed = normed_row(x_ref, affine_ref, k)
        proj = lax.dot_general(normed, weights, (((0,), (0,)), ((), ())), preferred_element_type=f32)
        out_ref[k] = 0.5 * jnp.tanh(0.5 * proj) + 0.5


def gate(place, x, gain, bias, w_gate, rows, after):
    _, width, chan = x.shape
    step = 8
    spec = pl.BlockSpec((step, width, chan), lambda i, _: (i, 0, 0))
    return call(
        gate_body,
        (rows // step,),
        [spec, whole((1, chan)), whole((1, chan)), whole(w_gate.shape)],
        spec,
        jax.ShapeDtypeStruct((rows, width, chan), f32),
        [pltpu.VMEM((2, chan, LANES), f32)],
        (2 * rows * width * chan * chan, 6 * rows * width * chan),
        (place, x, gain.reshape(1, chan), bias.reshape(1, chan), w_gate),
        after,
    )


def triangle_body(order, place, own_ref, got_ref, keep_ref, send_ref, hold):
    step, slots, block, _ = keep_ref.shape
    for h in range(step):
        left = jnp.concatenate([own_ref[0, h], got_ref[0, h]], axis=0)
        right = jnp.concatenate([own_ref[1, h], got_ref[1, h]], axis=0)
        hold[h] = lax.dot_general(left, right, (((0,), (0,)), ((), ())), preferred_element_type=f32)
        for slot in range(2 * slots):
            mask = 0
            for digit, bit in enumerate(reversed(order)):
                mask |= (slot >> digit & 1) << bit
            rows = pl.ds(pl.multiple_of((place[1] ^ mask) * block, block), block)
            if slot < slots:
                keep_ref[h, slot] = hold[h, rows, :]
            else:
                send_ref[h, slot - slots] = hold[h, rows, :].astype(bf16)


def triangle(place, own, got, order, after):
    _, size, depth, width = own.shape
    step = min(size, 4)
    slots = 2 ** (len(order) - 1)
    block = width // (2 * slots)
    spec = pl.BlockSpec((2, step, depth, width), lambda i, _: (0, i, 0, 0))
    out_spec = pl.BlockSpec((step, slots, block, width), lambda i, _: (i, 0, 0, 0))
    shape = (size, slots, block, width)
    return call(
        functools.partial(triangle_body, order),
        (size // step,),
        [spec, spec],
        [out_spec, out_spec],
        [jax.ShapeDtypeStruct(shape, f32), jax.ShapeDtypeStruct(shape, bf16)],
        [pltpu.VMEM((step, width, width), f32)],
        (4 * size * depth * width * width, 8 * size * depth * width + 3 * size * width * width),
        (place, own, got),
        after,
    )


def halve_body(place, held_ref, got_ref, keep_ref, send_ref):
    slots = keep_ref.shape[1]
    keep_ref[...] = held_ref[:, :slots] + got_ref[:, :slots].astype(f32)
    send_ref[...] = (held_ref[:, slots:] + got_ref[:, slots:].astype(f32)).astype(bf16)


def halve(place, held, got, after):
    size, slots, block, width = held.shape
    step = min(size, 4)
    spec = pl.BlockSpec((step, slots, block, width), lambda i, _: (i, 0, 0, 0))
    out_spec = pl.BlockSpec((step, slots // 2, block, width), lambda i, _: (i, 0, 0, 0))
    shape = (size, slots // 2, block, width)
    return call(
        halve_body,
        (size // step,),
        [spec, spec],
        [out_spec, out_spec],
        [jax.ShapeDtypeStruct(shape, f32), jax.ShapeDtypeStruct(shape, bf16)],
        [],
        (held.size, held.size * 9),
        (place, held, got),
        after,
    )


def total_body(place, held_ref, got_ref, mine_ref, theirs_ref, hold):
    hold[...] = held_ref[:, 0] + got_ref[:, 0].astype(f32)
    rows = mine_ref.shape[1]
    core = place[2]
    mine_ref[...] = hold[:, pl.ds(pl.multiple_of(core * rows, rows), rows), :]
    theirs_ref[...] = hold[:, pl.ds(pl.multiple_of((1 - core) * rows, rows), rows), :]


def total(place, held, got, after):
    size, _, block, width = held.shape
    spec = pl.BlockSpec((size, 1, block, width), lambda i, _: (i, 0, 0, 0))
    out_spec = pl.BlockSpec((size, block // 2, width), lambda i, _: (i, 0, 0))
    shape = jax.ShapeDtypeStruct((size, block // 2, width), f32)
    return call(
        total_body,
        (1,),
        [spec, spec],
        [out_spec] * 2,
        [shape, shape],
        [pltpu.VMEM((size, block, width), f32)],
        (held.size, held.size * 10),
        (place, held, got),
        after,
    )


def finish_body(chunks, place, *refs):
    count = len(chunks)
    mine, theirs = refs[:count], refs[count : 2 * count]
    gate_ref, gain_ref, bias_ref, w_ref, out_ref, hold = refs[2 * count :]
    hidden, _ = w_ref.shape
    half = hidden // 2
    _, rows, width = mine[0].shape
    stride = hold.shape[1] // hidden
    core = place[2]
    total_val = jnp.zeros((rows, width), f32)
    for part in mine + theirs:
        total_val = total_val + jnp.sum(part[...], axis=0)
    mean_val = total_val * (1.0 / hidden)
    square = jnp.zeros((rows, width), f32)
    for part in mine + theirs:
        for h in range(part.shape[0]):
            centered = part[h] - mean_val
            square = square + centered * centered
    scale = lax.rsqrt(square * (1.0 / hidden) + EPS)
    for owner, parts in ((0, mine), (1, theirs)):
        index = jnp.where(core == owner, 0, half)
        for part in parts:
            for h in range(part.shape[0]):
                value = (part[h] - mean_val) * scale * gain_ref[index] + bias_ref[index]
                for lane in range(width // LANES):
                    hold[lane, pl.ds(index * stride, rows), :] = value[:, lane * LANES : (lane + 1) * LANES]
                index = index + 1
    weights = w_ref[...]
    for row in range(rows):
        for lane in range(width // LANES):
            normed = hold[lane, pl.ds(row, hidden, stride=stride), :].astype(bf16)
            mixed = lax.dot_general(normed, weights, (((0,), (0,)), ((), ())), preferred_element_type=f32)
            span = pl.ds(lane * LANES, LANES)
            out_ref[row, span, :] = (gate_ref[row, span, :] * mixed).astype(bf16)


def finish(place, mine, theirs, gate_act, gain, bias, w_out):
    rows, width, chan = gate_act.shape
    hidden = w_out.shape[0]
    step = 8
    stride = step + 8
    parts = [pl.BlockSpec((part.shape[0], step, width), lambda i, _: (0, i, 0)) for part in mine]
    spec = pl.BlockSpec((step, width, chan), lambda i, _: (i, 0, 0))
    smem = pl.BlockSpec(memory_space=pltpu.SMEM)
    return call(
        functools.partial(finish_body, [part.shape[0] for part in mine]),
        (rows // step,),
        parts * 2 + [spec, smem, smem, whole(w_out.shape)],
        spec,
        jax.ShapeDtypeStruct((rows, width, chan), bf16),
        [pltpu.VMEM((width // LANES, hidden * stride, LANES), f32)],
        (2 * rows * width * chan * hidden, rows * width * (chan * 6 + hidden * 4)),
        (place, *mine, *theirs, gate_act, gain, bias, w_out),
    )


def event_order(sizes, orders, bits):
    links, order, flying = {}, [], []
    waiting = list(range(len(sizes)))

    def send(chunk, step, time):
        bit = orders[chunk][step]
        load = sizes[chunk] / 2**step
        link = min(bit, 1)
        begin = max(time, links.get(link, 0.0))
        links[link] = begin + load * max(bit, 1)
        flying.append((links[link] + 2.0, chunk, step))

    while waiting or flying:
        for chunk in [c for c in waiting if c < 2]:
            waiting.remove(chunk)
            order.append((chunk, 0))
            send(chunk, 0, 0.0)
        flying.sort()
        time, chunk, step = flying.pop(0)
        order.append((chunk, step + 1))
        if step + 1 < bits:
            send(chunk, step + 1, time + 2.0)
        if step == 0 and waiting:
            follower = waiting.pop(0)
            order.append((follower, 0))
            send(follower, 0, time + 2.0)
    return order


def on_device(pair_act, pair_mask, in_gain, in_bias, w_proj, w_gate, out_gain, out_bias, w_out):
    width = pair_act.shape[1]
    devices = lax.axis_size("row")
    bits = (devices // 2).bit_length() - 1
    half = w_out.shape[0] // 2
    chunks = (half // 4, half // 8, half // 4, half // 4, half // 8)
    z_last, z_first = tuple(range(bits)), tuple(range(1, bits)) + (0,)
    orders = tuple(z_first if c == 1 else z_last for c in range(len(chunks)))
    index = lax.axis_index("row")
    place = jnp.stack([index, index // 2, index % 2]).astype(jnp.int32)

    def swap(values, bit):
        return lax.ppermute(values, "row", [(d, d ^ bit) for d in range(devices)])

    last = []

    def put(kernel, *operands):
        outs = kernel(*operands, tuple(last[-1:]))
        last.append(outs[0] if isinstance(outs, (list, tuple)) else outs)
        return outs

    acts = put(project, place, pair_act, pair_mask, in_gain, in_bias, w_proj, chunks, 0, 56 * 2**20)
    count = len(chunks)
    own, got = acts[:count], [swap(part, 1) for part in acts[count:]]
    held, arrived = {}, {}

    def advance(chunk, step):
        if step == 0:
            held[chunk], sent = put(triangle, place, own[chunk], got[chunk], orders[chunk])
        elif step < bits:
            held[chunk], sent = put(halve, place, held[chunk], arrived[chunk])
        else:
            held[chunk], sent = put(total, place, held[chunk], arrived[chunk])
        arrived[chunk] = swap(sent, 2 << orders[chunk][step] if step < bits else 1)

    sizes = [11.4 * size / (half // 4) for size in chunks]
    for position, (chunk, step) in enumerate(event_order(sizes, orders, bits)):
        advance(chunk, step)
        if position == 1:
            gate_act = put(gate, place, pair_act, in_gain, in_bias, w_gate, width // devices)
    mine, theirs = [held[c] for c in range(count)], [arrived[c] for c in range(count)]
    return finish(place, mine, theirs, gate_act, out_gain, out_bias, w_out)


def solution(mesh):
    return jax.shard_map(
        on_device,
        mesh=mesh,
        in_specs=(
            P(("groups", "row"), None, None),
            P(("groups", "row"), None),
            P(),
            P(),
            P(),
            P(),
            P(),
            P(),
            P(),
        ),
        out_specs=P(("groups", "row"), None, None),
        check_vma=False,
    )
```

```python
import functools

import jax
import jax.numpy as jnp
from jax import lax
from jax.experimental import pallas as pl
from jax.experimental.pallas import tpu as pltpu
from jax.sharding import PartitionSpec as P

f32 = jnp.float32
bf16 = jnp.bfloat16
LANES = 128
EPS = 1e-05
VMEM_BYTES = 12 << 20
PROJECT_ROWS = 16
IN_PLACE = pl.BlockSpec(memory_space=pltpu.VMEM)


def whole(shape):
    return pl.BlockSpec(shape, lambda *_: (0,) * len(shape))


def corner(shape):
    return pl.BlockSpec((1,) * (len(shape) - 2) + (16, LANES), lambda *_: (0,) * len(shape))


def call(body, grid, in_specs, out_specs, out_shape, scratch, cost, operands, after=(), vmem=VMEM_BYTES):
    count = len(operands)
    extra = len(after)

    def run(*refs):
        return body(*refs[:count], *refs[count + extra :])

    return pl.pallas_call(
        run,
        grid=grid,
        in_specs=list(in_specs) + [corner(array.shape) for array in after],
        out_specs=out_specs,
        out_shape=out_shape,
        scratch_shapes=scratch,
        compiler_params=pltpu.CompilerParams(vmem_limit_bytes=vmem),
        cost_estimate=pl.CostEstimate(flops=cost[0], bytes_accessed=cost[1], transcendentals=0),
    )(*operands, *after)


def norm_columns(tile, gain, bias):
    count = tile.shape[0]
    mean_val = jnp.sum(tile, axis=0, keepdims=True) * (1.0 / count)
    centered = tile - mean_val
    variance = jnp.sum(centered * centered, axis=0, keepdims=True) * (1.0 / count)
    return (centered * lax.rsqrt(variance + EPS) * gain + bias).astype(bf16)


def gather_weights(w_ref, wt_ref):
    hidden = w_ref.shape[1] // 4
    turned = w_ref[...].astype(f32).T * 0.5
    for value in range(2):
        for side in range(2):
            source, target = (2 * side + value) * hidden, (2 * value + side) * hidden
            wt_ref[target : target + hidden, :] = turned[source : source + hidden].astype(bf16)


def turn_affine(gain_ref, bias_ref, affine_ref):
    chan = gain_ref.shape[1]
    affine_ref[0] = jnp.broadcast_to(gain_ref[...], (LANES, chan)).T
    affine_ref[1] = jnp.broadcast_to(bias_ref[...], (LANES, chan)).T


def normed_row(x_ref, affine_ref, k):
    parts = [
        norm_columns(x_ref[k, low : low + LANES, :].T.astype(f32), affine_ref[0], affine_ref[1])
        for low in range(0, x_ref.shape[1], LANES)
    ]
    return jnp.concatenate(parts, axis=1)


def project_body(chunks, stride, all_ref, all_mask, all_gain, all_bias, all_w, *rest):
    count = len(chunks)
    outs, rest = (rest[:count], rest[count : 2 * count]), rest[2 * count :]
    window_ref, hold, wt_ref, affine_ref, x_buf, mask_ref, gain_ref, bias_ref, w_ref, x_sem, sems = rest
    _, rows, width, _ = x_buf.shape
    size = sum(chunks)
    step, steps = pl.program_id(0), all_ref.shape[0] // rows

    def fetch(number):
        slot = number % 2
        block = all_ref.at[pl.ds(number * rows, rows)]
        return pltpu.make_async_copy(block, x_buf.at[slot], x_sem.at[slot])

    window = pltpu.make_async_copy(all_ref.at[pl.ds(0, window_ref.shape[0])], window_ref, sems.at[4])

    @pl.when(step == 0)
    def _():
        pairs = ((all_w, w_ref), (all_gain, gain_ref), (all_bias, bias_ref), (all_mask, mask_ref))
        copies = [pltpu.make_async_copy(source, target, sems.at[n]) for n, (source, target) in enumerate(pairs)]
        fetch(0).start()
        for copy in copies:
            copy.start()
        window.start()
        for copy in copies:
            copy.wait()
        gather_weights(w_ref, wt_ref)
        turn_affine(gain_ref, bias_ref, affine_ref)

    @pl.when(step + 1 < steps)
    def _():
        fetch(step + 1).start()

    @pl.when(step + 1 == steps)
    def _():
        window.wait()

    weights = wt_ref[...]
    fetch(step).wait()
    x_ref = x_buf.at[step % 2]
    for k in range(rows):
        proj = jnp.dot(weights, normed_row(x_ref, affine_ref, k), preferred_element_type=f32)
        keep = mask_ref[pl.ds(step * rows + k, 1), :].astype(f32)
        act = (jnp.tanh(proj[: 4 * size]) + 1.0) * proj[4 * size :] * keep
        for lane in range(width // LANES):
            hold[lane, pl.ds(k * stride, 4 * size), :] = act[:, lane * LANES : (lane + 1) * LANES]
    span = pl.ds(pl.multiple_of(step * rows, rows), rows)
    for owner in range(2):
        base = jnp.where(lax.axis_index("row") % 2 == owner, 0, size)
        offset = 0
        for out, count in zip(outs[owner], chunks):
            for side in range(2):
                for h in range(count):
                    for lane in range(width // LANES):
                        start = base + 2 * side * size + offset + h
                        tile = hold[lane, pl.ds(start, rows, stride=stride), :]
                        out[side, h, span, lane * LANES : (lane + 1) * LANES] = tile.astype(bf16)
            offset += count


def project(x, mask, gain, bias, w_proj, chunks, window, vmem, after):
    depth, width, chan = x.shape
    rows, size = PROJECT_ROWS, sum(chunks)
    stride = 4 * size + 4
    return call(
        functools.partial(project_body, chunks, stride),
        (depth // rows,),
        [pl.BlockSpec(memory_space=pltpu.HBM)] * 5,
        [IN_PLACE] * (2 * len(chunks) + 1),
        [pltpu.VMEM((2, size, depth, width), bf16) for size in chunks] * 2 + [pltpu.VMEM((window, width, chan), bf16)],
        [
            pltpu.VMEM((width // LANES, rows * stride, LANES), f32),
            pltpu.VMEM((8 * size, chan), bf16),
            pltpu.VMEM((2, chan, LANES), f32),
            pltpu.VMEM((2, rows, width, chan), bf16),
            pltpu.VMEM((depth, width), mask.dtype),
            pltpu.VMEM((1, chan), f32),
            pltpu.VMEM((1, chan), f32),
            pltpu.VMEM(w_proj.shape, bf16),
            pltpu.SemaphoreType.DMA((2,)),
            pltpu.SemaphoreType.DMA((5,)),
        ],
        (2 * depth * width * chan * 8 * size, 4 * depth * width * chan),
        (x, mask, gain.reshape(1, chan), bias.reshape(1, chan), w_proj),
        after,
        vmem,
    )


def gate_body(x_ref, gain_ref, bias_ref, w_ref, out_ref, affine_ref):
    turn_affine(gain_ref, bias_ref, affine_ref)
    weights = w_ref[...]
    for k in range(x_ref.shape[0]):
        normed = normed_row(x_ref, affine_ref, k)
        proj = lax.dot_general(normed, weights, (((0,), (0,)), ((), ())), preferred_element_type=f32)
        out_ref[k] = 0.5 * jnp.tanh(0.5 * proj) + 0.5


def gate(x, gain, bias, w_gate, after):
    rows, width, chan = x.shape
    return call(
        gate_body,
        (1,),
        [IN_PLACE] * 4,
        IN_PLACE,
        pltpu.VMEM(x.shape, f32),
        [pltpu.VMEM((2, chan, LANES), f32)],
        (2 * rows * width * chan * chan, 6 * rows * width * chan),
        (x, gain.reshape(1, chan), bias.reshape(1, chan), w_gate),
        after,
    )


def triangle_body(order, own_ref, got_ref, keep_ref, send_ref, hold):
    count, slots, block, _ = keep_ref.shape
    device = lax.axis_index("row")
    for h in range(count):
        left = jnp.concatenate([own_ref[0, h], got_ref[0, h]], axis=0)
        right = jnp.concatenate([own_ref[1, h], got_ref[1, h]], axis=0)
        hold[h % 4] = lax.dot_general(left, right, (((0,), (0,)), ((), ())), preferred_element_type=f32)
        for slot in range(2 * slots):
            mask = 0
            for digit, bit in enumerate(reversed(order)):
                mask |= (slot >> digit & 1) << bit
            rows = pl.ds(pl.multiple_of((device ^ mask) // 2 * block, block), block)
            if slot < slots:
                keep_ref[h, slot] = hold[h % 4, rows, :]
            else:
                send_ref[h, slot - slots] = hold[h % 4, rows, :].astype(bf16)


def triangle(own, got, order, after):
    _, size, depth, width = own.shape
    slots = 2 ** (len(order) - 1)
    shape = (size, slots, width // (2 * slots), width)
    return call(
        functools.partial(triangle_body, order),
        (1,),
        [IN_PLACE] * 2,
        [IN_PLACE] * 2,
        [pltpu.VMEM(shape, f32), pltpu.VMEM(shape, bf16)],
        [pltpu.VMEM((4, width, width), f32)],
        (4 * size * depth * width * width, 8 * size * depth * width + 3 * size * width * width),
        (own, got),
        after,
    )


def halve_body(held_ref, got_ref, keep_ref, send_ref):
    slots = keep_ref.shape[1]
    keep_ref[...] = held_ref[:, :slots] + got_ref[:, :slots].astype(f32)
    send_ref[...] = (held_ref[:, slots:] + got_ref[:, slots:].astype(f32)).astype(bf16)


def halve(held, got, after):
    count, slots, block, width = held.shape
    shape = (count, slots // 2, block, width)
    return call(
        halve_body,
        (1,),
        [IN_PLACE] * 2,
        [IN_PLACE] * 2,
        [pltpu.VMEM(shape, f32), pltpu.VMEM(shape, bf16)],
        [],
        (held.size, held.size * 9),
        (held, got),
        after,
    )


def total_body(held_ref, got_ref, mine_ref, theirs_ref, hold):
    hold[...] = held_ref[:, 0] + got_ref[:, 0].astype(f32)
    rows = mine_ref.shape[1]
    core = lax.axis_index("row") % 2
    mine_ref[...] = hold[:, pl.ds(pl.multiple_of(core * rows, rows), rows), :]
    theirs_ref[...] = hold[:, pl.ds(pl.multiple_of((1 - core) * rows, rows), rows), :]


def total(held, got, after):
    count, _, block, width = held.shape
    shape = pltpu.VMEM((count, block // 2, width), f32)
    return call(
        total_body,
        (1,),
        [IN_PLACE] * 2,
        [IN_PLACE] * 2,
        [shape, shape],
        [pltpu.VMEM((count, block, width), f32)],
        (held.size, held.size * 10),
        (held, got),
        after,
    )


def finish_body(chunks, *refs):
    count = len(chunks)
    mine, theirs = refs[:count], refs[count : 2 * count]
    gate_ref, gain_ref, bias_ref, w_ref, out_ref, hold = refs[2 * count :]
    hidden, _ = w_ref.shape
    half = hidden // 2
    rows, width, _ = gate_ref.shape
    stride = hold.shape[1] // hidden
    core = lax.axis_index("row") % 2

    @pl.when(pl.program_id(0) == 0)
    def _():
        sums = []
        first = 0
        for chunk, size in enumerate(chunks):
            for part in range(2):
                for h in range(size):
                    index = jnp.where(core == part, 0, half) + first + h
                    sums.append((index, (mine, theirs)[part][chunk][h]))
            first += size
        mean_val = sum(value for _, value in sums) * (1.0 / hidden)
        square = sum((value - mean_val) * (value - mean_val) for _, value in sums)
        scale = lax.rsqrt(square * (1.0 / hidden) + EPS)
        for index, value in sums:
            value = (value - mean_val) * scale * gain_ref[index] + bias_ref[index]
            for lane in range(width // LANES):
                hold[lane, pl.ds(index * stride, rows), :] = value[:, lane * LANES : (lane + 1) * LANES]

    weights = w_ref[...]
    for near in range(out_ref.shape[0]):
        row = pl.program_id(0) * out_ref.shape[0] + near
        for lane in range(width // LANES):
            normed = hold[lane, pl.ds(row, hidden, stride=stride), :].astype(bf16)
            mixed = lax.dot_general(normed, weights, (((0,), (0,)), ((), ())), preferred_element_type=f32)
            span = pl.ds(lane * LANES, LANES)
            out_ref[near, span, :] = (gate_ref[row, span, :] * mixed).astype(bf16)


def finish(mine, theirs, gate_act, gain, bias, w_out, chunks):
    rows, width, chan = gate_act.shape
    hidden = w_out.shape[0]
    step = 4
    stride = rows + 4
    smem = pl.BlockSpec(memory_space=pltpu.SMEM)
    return call(
        functools.partial(finish_body, chunks),
        (rows // step,),
        [IN_PLACE] * (2 * len(mine) + 1) + [smem, smem, IN_PLACE],
        pl.BlockSpec((step, width, chan), lambda i: (i, 0, 0)),
        jax.ShapeDtypeStruct((rows, width, chan), bf16),
        [pltpu.VMEM((width // LANES, hidden * stride, LANES), f32)],
        (2 * rows * width * chan * hidden, rows * width * (chan * 6 + hidden * 4)),
        (*mine, *theirs, gate_act, gain, bias, w_out),
    )


def in_turn(orders):
    events, turn = [], 0
    for chunk, order in enumerate(orders):
        late = order[0] != 1
        for step in range(len(order) + 1):
            if late:
                time = step + (step == len(order))
            else:
                time = turn + step if step else max(turn - 1, 0)
            events.append((time, step == 0, late and step > 0, step, chunk))
        turn += not late
    return [(chunk, step) for *_, step, chunk in sorted(events)]


def on_device(pair_act, pair_mask, in_gain, in_bias, w_proj, w_gate, out_gain, out_bias, w_out):
    width = pair_act.shape[1]
    devices = lax.axis_size("row")
    bits = devices.bit_length() - 1
    unit = w_out.shape[0] // 32
    z_last, z_first = tuple(range(1, bits)), tuple(range(2, bits)) + (1,)
    plan = ((4, z_last), (2, z_first), (4, z_last), (3, z_last), (2, z_last), (1, z_last))
    chunks, orders = tuple(size * unit for size, _ in plan), tuple(order for _, order in plan)
    count = len(chunks)

    def swap(values, bit):
        return lax.ppermute(values, "row", [(d, d ^ 1 << bit) for d in range(devices)])

    last = []

    def put(kernel, *operands):
        outs = kernel(*operands, tuple(last[-1:]))
        last.append(outs[0] if isinstance(outs, (list, tuple)) else outs)
        return outs

    vmem = (61 << 20) - pair_act.shape[0] * width * w_out.shape[0] * 4
    acts = put(
        project, pair_act, pair_mask, in_gain, in_bias, w_proj, chunks, width // devices, vmem
    )
    own, got = acts[:count], [swap(part, 0) for part in acts[count:-1]]
    held, arrived = {}, {}

    def advance(chunk, step):
        order = orders[chunk]
        if step == 0:
            held[chunk], sent = put(triangle, own[chunk], got[chunk], order)
        elif step < len(order):
            held[chunk], sent = put(halve, held[chunk], arrived[chunk])
        else:
            held[chunk], sent = put(total, held[chunk], arrived[chunk])
        arrived[chunk] = swap(sent, order[step] if step < len(order) else 0)

    sequence = in_turn(orders)
    for position, (chunk, step) in enumerate(sequence):
        with jax.named_scope(f"chunk{chunk}_step{step}"):
            advance(chunk, step)
        if position == 1:
            gate_act = put(gate, acts[-1], in_gain, in_bias, w_gate)
    mine, theirs = [held[c] for c in range(count)], [arrived[c] for c in range(count)]
    return finish(mine, theirs, gate_act, out_gain, out_bias, w_out, chunks)


def solution(mesh):
    return jax.shard_map(
        on_device,
        mesh=mesh,
        in_specs=(
            P(("groups", "row"), None, None),
            P(("groups", "row"), None),
            P(),
            P(),
            P(),
            P(),
            P(),
            P(),
            P(),
        ),
        out_specs=P(("groups", "row"), None, None),
        check_vma=False,
    )
```

```python
import functools

import jax
import jax.numpy as jnp
from jax import lax
from jax.experimental import pallas as pl
from jax.experimental.pallas import tpu as pltpu
from jax.sharding import PartitionSpec as P

f32 = jnp.float32
bf16 = jnp.bfloat16
LANES = 128
EPS = 1e-05
VMEM_BYTES = 12 << 20
PROJECT_ROWS = 16
IN_PLACE = pl.BlockSpec(memory_space=pltpu.VMEM)


def whole(shape):
    return pl.BlockSpec(shape, lambda *_: (0,) * len(shape))


def corner(shape):
    return pl.BlockSpec((1,) * (len(shape) - 2) + (16, LANES), lambda *_: (0,) * len(shape))


def call(body, grid, in_specs, out_specs, out_shape, scratch, cost, operands, after=(), vmem=VMEM_BYTES):
    count = len(operands)
    extra = len(after)

    def run(*refs):
        return body(*refs[:count], *refs[count + extra :])

    return pl.pallas_call(
        run,
        grid=grid,
        in_specs=list(in_specs) + [corner(array.shape) for array in after],
        out_specs=out_specs,
        out_shape=out_shape,
        scratch_shapes=scratch,
        compiler_params=pltpu.CompilerParams(vmem_limit_bytes=vmem),
        cost_estimate=pl.CostEstimate(flops=cost[0], bytes_accessed=cost[1], transcendentals=0),
    )(*operands, *after)


def norm_columns(tile, gain, bias):
    count = tile.shape[0]
    mean_val = jnp.sum(tile, axis=0, keepdims=True) * (1.0 / count)
    centered = tile - mean_val
    variance = jnp.sum(centered * centered, axis=0, keepdims=True) * (1.0 / count)
    return (centered * lax.rsqrt(variance + EPS) * gain + bias).astype(bf16)


def gather_weights(w_ref, wt_ref):
    hidden = w_ref.shape[1] // 4
    turned = w_ref[...].astype(f32).T * 0.5
    for value in range(2):
        for side in range(2):
            source, target = (2 * side + value) * hidden, (2 * value + side) * hidden
            wt_ref[target : target + hidden, :] = turned[source : source + hidden].astype(bf16)


def turn_affine(gain_ref, bias_ref, affine_ref):
    chan = gain_ref.shape[1]
    affine_ref[0] = jnp.broadcast_to(gain_ref[...], (LANES, chan)).T
    affine_ref[1] = jnp.broadcast_to(bias_ref[...], (LANES, chan)).T


def normed_row(x_ref, affine_ref, k):
    parts = [
        norm_columns(x_ref[k, low : low + LANES, :].T.astype(f32), affine_ref[0], affine_ref[1])
        for low in range(0, x_ref.shape[1], LANES)
    ]
    return jnp.concatenate(parts, axis=1)


def project_body(chunks, stride, all_ref, all_mask, all_gain, all_bias, all_w, *rest):
    count = len(chunks)
    outs, rest = (rest[:count], rest[count : 2 * count]), rest[2 * count :]
    window_ref, hold, wt_ref, affine_ref, x_buf, mask_ref, gain_ref, bias_ref, w_ref, x_sem, sems = rest
    _, rows, width, _ = x_buf.shape
    size = sum(chunks)
    step, steps = pl.program_id(0), all_ref.shape[0] // rows

    def fetch(number):
        slot = number % 2
        block = all_ref.at[pl.ds(number * rows, rows)]
        return pltpu.make_async_copy(block, x_buf.at[slot], x_sem.at[slot])

    window = pltpu.make_async_copy(all_ref.at[pl.ds(0, window_ref.shape[0])], window_ref, sems.at[4])

    @pl.when(step == 0)
    def _():
        pairs = ((all_w, w_ref), (all_gain, gain_ref), (all_bias, bias_ref), (all_mask, mask_ref))
        copies = [pltpu.make_async_copy(source, target, sems.at[n]) for n, (source, target) in enumerate(pairs)]
        fetch(0).start()
        for copy in copies:
            copy.start()
        window.start()
        for copy in copies:
            copy.wait()
        gather_weights(w_ref, wt_ref)
        turn_affine(gain_ref, bias_ref, affine_ref)

    @pl.when(step + 1 < steps)
    def _():
        fetch(step + 1).start()

    @pl.when(step + 1 == steps)
    def _():
        window.wait()

    weights = wt_ref[...]
    fetch(step).wait()
    x_ref = x_buf.at[step % 2]
    for k in range(rows):
        proj = jnp.dot(weights, normed_row(x_ref, affine_ref, k), preferred_element_type=f32)
        keep = mask_ref[pl.ds(step * rows + k, 1), :].astype(f32)
        act = (jnp.tanh(proj[: 4 * size]) + 1.0) * proj[4 * size :] * keep
        for lane in range(width // LANES):
            hold[lane, pl.ds(k * stride, 4 * size), :] = act[:, lane * LANES : (lane + 1) * LANES]
    span = pl.ds(pl.multiple_of(step * rows, rows), rows)
    for owner in range(2):
        base = jnp.where(lax.axis_index("row") % 2 == owner, 0, size)
        offset = 0
        for out, count in zip(outs[owner], chunks):
            for side in range(2):
                for h in range(count):
                    for lane in range(width // LANES):
                        start = base + 2 * side * size + offset + h
                        tile = hold[lane, pl.ds(start, rows, stride=stride), :]
                        out[side, h, span, lane * LANES : (lane + 1) * LANES] = tile.astype(bf16)
            offset += count


def project(x, mask, gain, bias, w_proj, chunks, window, vmem, after):
    depth, width, chan = x.shape
    rows, size = PROJECT_ROWS, sum(chunks)
    stride = 4 * size + 4
    return call(
        functools.partial(project_body, chunks, stride),
        (depth // rows,),
        [pl.BlockSpec(memory_space=pltpu.HBM)] * 5,
        [IN_PLACE] * (2 * len(chunks) + 1),
        [pltpu.VMEM((2, size, depth, width), bf16) for size in chunks] * 2 + [pltpu.VMEM((window, width, chan), bf16)],
        [
            pltpu.VMEM((width // LANES, rows * stride, LANES), f32),
            pltpu.VMEM((8 * size, chan), bf16),
            pltpu.VMEM((2, chan, LANES), f32),
            pltpu.VMEM((2, rows, width, chan), bf16),
            pltpu.VMEM((depth, width), mask.dtype),
            pltpu.VMEM((1, chan), f32),
            pltpu.VMEM((1, chan), f32),
            pltpu.VMEM(w_proj.shape, bf16),
            pltpu.SemaphoreType.DMA((2,)),
            pltpu.SemaphoreType.DMA((5,)),
        ],
        (2 * depth * width * chan * 8 * size, 4 * depth * width * chan),
        (x, mask, gain.reshape(1, chan), bias.reshape(1, chan), w_proj),
        after,
        vmem,
    )


def gate_body(x_ref, gain_ref, bias_ref, w_ref, out_ref, affine_ref):
    turn_affine(gain_ref, bias_ref, affine_ref)
    weights = w_ref[...]
    for k in range(x_ref.shape[0]):
        normed = normed_row(x_ref, affine_ref, k)
        proj = lax.dot_general(normed, weights, (((0,), (0,)), ((), ())), preferred_element_type=f32)
        out_ref[k] = 0.5 * jnp.tanh(0.5 * proj) + 0.5


def gate(x, gain, bias, w_gate, after):
    rows, width, chan = x.shape
    return call(
        gate_body,
        (1,),
        [IN_PLACE] * 4,
        IN_PLACE,
        pltpu.VMEM(x.shape, f32),
        [pltpu.VMEM((2, chan, LANES), f32)],
        (2 * rows * width * chan * chan, 6 * rows * width * chan),
        (x, gain.reshape(1, chan), bias.reshape(1, chan), w_gate),
        after,
    )


def triangle_body(order, own_ref, got_ref, keep_ref, send_ref, hold):
    count, slots, block, _ = keep_ref.shape
    device = lax.axis_index("row")
    for h in range(count):
        left = jnp.concatenate([own_ref[0, h], got_ref[0, h]], axis=0)
        right = jnp.concatenate([own_ref[1, h], got_ref[1, h]], axis=0)
        hold[h % 4] = lax.dot_general(left, right, (((0,), (0,)), ((), ())), preferred_element_type=f32)
        for slot in range(2 * slots):
            mask = 0
            for digit, bit in enumerate(reversed(order)):
                mask |= (slot >> digit & 1) << bit
            rows = pl.ds(pl.multiple_of((device ^ mask) // 2 * block, block), block)
            if slot < slots:
                keep_ref[h, slot] = hold[h % 4, rows, :]
            else:
                send_ref[h, slot - slots] = hold[h % 4, rows, :].astype(bf16)


def triangle(own, got, order, after):
    _, size, depth, width = own.shape
    slots = 2 ** (len(order) - 1)
    shape = (size, slots, width // (2 * slots), width)
    return call(
        functools.partial(triangle_body, order),
        (1,),
        [IN_PLACE] * 2,
        [IN_PLACE] * 2,
        [pltpu.VMEM(shape, f32), pltpu.VMEM(shape, bf16)],
        [pltpu.VMEM((4, width, width), f32)],
        (4 * size * depth * width * width, 8 * size * depth * width + 3 * size * width * width),
        (own, got),
        after,
    )


def halve_body(held_ref, got_ref, keep_ref, send_ref):
    slots = keep_ref.shape[1]
    keep_ref[...] = held_ref[:, :slots] + got_ref[:, :slots].astype(f32)
    send_ref[...] = (held_ref[:, slots:] + got_ref[:, slots:].astype(f32)).astype(bf16)


def halve(held, got, after):
    count, slots, block, width = held.shape
    shape = (count, slots // 2, block, width)
    return call(
        halve_body,
        (1,),
        [IN_PLACE] * 2,
        [IN_PLACE] * 2,
        [pltpu.VMEM(shape, f32), pltpu.VMEM(shape, bf16)],
        [],
        (held.size, held.size * 9),
        (held, got),
        after,
    )


def total_body(held_ref, got_ref, mine_ref, theirs_ref, hold):
    hold[...] = held_ref[:, 0] + got_ref[:, 0].astype(f32)
    rows = mine_ref.shape[1]
    core = lax.axis_index("row") % 2
    mine_ref[...] = hold[:, pl.ds(pl.multiple_of(core * rows, rows), rows), :]
    theirs_ref[...] = hold[:, pl.ds(pl.multiple_of((1 - core) * rows, rows), rows), :]


def total(held, got, after):
    count, _, block, width = held.shape
    shape = pltpu.VMEM((count, block // 2, width), f32)
    return call(
        total_body,
        (1,),
        [IN_PLACE] * 2,
        [IN_PLACE] * 2,
        [shape, shape],
        [pltpu.VMEM((count, block, width), f32)],
        (held.size, held.size * 10),
        (held, got),
        after,
    )


def finish_body(chunks, *refs):
    count = len(chunks)
    parts = refs[:count], refs[count : 2 * count]
    gate_ref, gain_ref, bias_ref, w_ref, all_ref, hold, wide_ref, out_ref, sems = refs[2 * count :]
    hidden, chan = w_ref.shape
    half = hidden // 2
    rows, width, _ = gate_ref.shape
    stride = hold.shape[1] // hidden

    values = [part[h] for side in parts for part in side for h in range(part.shape[0])]
    mean_val = sum(values) * (1.0 / hidden)
    square = sum((value - mean_val) * (value - mean_val) for value in values)
    scale = lax.rsqrt(square * (1.0 / hidden) + EPS)
    base = lax.axis_index("row") % 2 * half
    for place, value in enumerate(values):
        index = base + place if place < half else place - base
        value = (value - mean_val) * scale * gain_ref[index] + bias_ref[index]
        for lane in range(width // LANES):
            hold[lane, place * stride : place * stride + rows, :] = value[:, lane * LANES : (lane + 1) * LANES]
    wide_ref[...] = jnp.zeros_like(wide_ref)
    for place, start in ((0, base), (half, half - base)):
        block = w_ref[pl.ds(pl.multiple_of(start, half), half), :]
        wide_ref[place : place + half, :chan] = block
        wide_ref[hidden + place : hidden + place + half, chan:] = block

    weights = wide_ref[...]
    copies = []
    for row in range(0, rows, 2):
        for lane in range(width // LANES):
            pair = [hold[lane, pl.ds(row + n, hidden, stride=stride), :].astype(bf16) for n in range(2)]
            normed = jnp.concatenate(pair, axis=0)
            mixed = lax.dot_general(normed, weights, (((0,), (0,)), ((), ())), preferred_element_type=f32)
            span = pl.ds(lane * LANES, LANES)
            for n in range(2):
                value = gate_ref[row + n, span, :] * mixed[:, n * chan : (n + 1) * chan]
                out_ref[row + n, span, :] = value.astype(bf16)
        if row % 4 == 2:
            block = pl.ds(row - 2, 4)
            copies.append(pltpu.make_async_copy(out_ref.at[block], all_ref.at[block], sems.at[row // 4]))
            copies[-1].start()
    for copy in copies:
        copy.wait()


def finish(mine, theirs, gate_act, gain, bias, w_out, chunks):
    rows, width, chan = gate_act.shape
    hidden = w_out.shape[0]
    stride = rows + 8
    smem = pl.BlockSpec(memory_space=pltpu.SMEM)
    return call(
        functools.partial(finish_body, chunks),
        (1,),
        [IN_PLACE] * (2 * len(mine) + 1) + [smem, smem, IN_PLACE],
        pl.BlockSpec(memory_space=pltpu.HBM),
        jax.ShapeDtypeStruct((rows, width, chan), bf16),
        [
            pltpu.VMEM((width // LANES, hidden * stride, LANES), f32),
            pltpu.VMEM((2 * hidden, 2 * chan), bf16),
            pltpu.VMEM((rows, width, chan), bf16),
            pltpu.SemaphoreType.DMA((rows // 4,)),
        ],
        (2 * rows * width * chan * hidden, rows * width * (chan * 6 + hidden * 4)),
        (*mine, *theirs, gate_act, gain, bias, w_out),
    )


def in_turn(orders):
    events, turn = [], 0
    for chunk, order in enumerate(orders):
        late = order[0] != 1
        for step in range(len(order) + 1):
            if late:
                time = step + 2 * (step == len(order))
            else:
                time = turn + step if step else max(turn - 1, 0)
            events.append((time, step == 0, late and step > 0, step, chunk))
        turn += not late
    return [(chunk, step) for *_, step, chunk in sorted(events)]


def on_device(pair_act, pair_mask, in_gain, in_bias, w_proj, w_gate, out_gain, out_bias, w_out):
    width = pair_act.shape[1]
    devices = lax.axis_size("row")
    bits = devices.bit_length() - 1
    unit = w_out.shape[0] // 32
    z_last, z_first = tuple(range(1, bits)), tuple(range(2, bits)) + (1,)
    plan = ((4, z_last), (3, z_first), (4, z_last), (3, z_last), (2, z_last))
    chunks, orders = tuple(size * unit for size, _ in plan), tuple(order for _, order in plan)
    count = len(chunks)

    def swap(values, bit):
        return lax.ppermute(values, "row", [(d, d ^ 1 << bit) for d in range(devices)])

    last = []

    def put(kernel, *operands):
        outs = kernel(*operands, tuple(last[-1:]))
        last.append(outs[0] if isinstance(outs, (list, tuple)) else outs)
        return outs

    vmem = (61 << 20) - pair_act.shape[0] * width * w_out.shape[0] * 4
    acts = put(
        project, pair_act, pair_mask, in_gain, in_bias, w_proj, chunks, width // devices, vmem
    )
    own, got = acts[:count], [swap(part, 0) for part in acts[count:-1]]
    held, arrived = {}, {}

    def advance(chunk, step):
        order = orders[chunk]
        if step == 0:
            held[chunk], sent = put(triangle, own[chunk], got[chunk], order)
        elif step < len(order):
            held[chunk], sent = put(halve, held[chunk], arrived[chunk])
        else:
            held[chunk], sent = put(total, held[chunk], arrived[chunk])
        arrived[chunk] = swap(sent, order[step] if step < len(order) else 0)

    sequence = in_turn(orders)
    for position, (chunk, step) in enumerate(sequence):
        with jax.named_scope(f"chunk{chunk}_step{step}"):
            advance(chunk, step)
        if position == 1:
            gate_act = put(gate, acts[-1], in_gain, in_bias, w_gate)
    mine, theirs = [held[c] for c in range(count)], [arrived[c] for c in range(count)]
    return finish(mine, theirs, gate_act, out_gain, out_bias, w_out, chunks)


def solution(mesh):
    return jax.shard_map(
        on_device,
        mesh=mesh,
        in_specs=(
            P(("groups", "row"), None, None),
            P(("groups", "row"), None),
            P(),
            P(),
            P(),
            P(),
            P(),
            P(),
            P(),
        ),
        out_specs=P(("groups", "row"), None, None),
        check_vma=False,
    )
```

```python
import functools

import jax
import jax.numpy as jnp
from jax import lax
from jax.experimental import pallas as pl
from jax.experimental.pallas import tpu as pltpu
from jax.sharding import PartitionSpec as P

f32 = jnp.float32
bf16 = jnp.bfloat16
LANES = 128
EPS = 1e-05
VMEM_BYTES = 12 << 20
PROJECT_ROWS = 16
IN_PLACE = pl.BlockSpec(memory_space=pltpu.VMEM)


def whole(shape):
    return pl.BlockSpec(shape, lambda *_: (0,) * len(shape))


def corner(shape):
    return pl.BlockSpec((1,) * (len(shape) - 2) + (16, LANES), lambda *_: (0,) * len(shape))


def call(body, grid, in_specs, out_specs, out_shape, scratch, cost, operands, after=(), vmem=VMEM_BYTES):
    count = len(operands)
    extra = len(after)

    def run(*refs):
        return body(*refs[:count], *refs[count + extra :])

    return pl.pallas_call(
        run,
        grid=grid,
        in_specs=list(in_specs) + [corner(array.shape) for array in after],
        out_specs=out_specs,
        out_shape=out_shape,
        scratch_shapes=scratch,
        compiler_params=pltpu.CompilerParams(vmem_limit_bytes=vmem),
        cost_estimate=pl.CostEstimate(flops=cost[0], bytes_accessed=cost[1], transcendentals=0),
    )(*operands, *after)


def norm_columns(tile, gain, bias):
    count = tile.shape[0]
    mean_val = jnp.sum(tile, axis=0, keepdims=True) * (1.0 / count)
    centered = tile - mean_val
    variance = jnp.sum(centered * centered, axis=0, keepdims=True) * (1.0 / count)
    return (centered * lax.rsqrt(variance + EPS) * gain + bias).astype(bf16)


def gather_weights(w_ref, wt_ref):
    hidden = w_ref.shape[1] // 4
    turned = w_ref[...].astype(f32).T * 0.5
    for value in range(2):
        for side in range(2):
            source, target = (2 * side + value) * hidden, (2 * value + side) * hidden
            wt_ref[target : target + hidden, :] = turned[source : source + hidden].astype(bf16)


def turn_affine(gain_ref, bias_ref, affine_ref):
    chan = gain_ref.shape[1]
    affine_ref[0] = jnp.broadcast_to(gain_ref[...], (LANES, chan)).T
    affine_ref[1] = jnp.broadcast_to(bias_ref[...], (LANES, chan)).T


def normed_row(x_ref, affine_ref, k):
    parts = [
        norm_columns(x_ref[k, low : low + LANES, :].T.astype(f32), affine_ref[0], affine_ref[1])
        for low in range(0, x_ref.shape[1], LANES)
    ]
    return jnp.concatenate(parts, axis=1)


def project_body(chunks, stride, all_ref, all_mask, all_gain, all_bias, all_w, *rest):
    count = len(chunks)
    outs, rest = (rest[:count], rest[count : 2 * count]), rest[2 * count :]
    window_ref, hold, wt_ref, affine_ref, x_buf, mask_ref, gain_ref, bias_ref, w_ref, x_sem, sems = rest
    _, rows, width, _ = x_buf.shape
    size = sum(chunks)
    step, steps = pl.program_id(0), all_ref.shape[0] // rows

    def fetch(number):
        slot = number % 2
        block = all_ref.at[pl.ds(number * rows, rows)]
        return pltpu.make_async_copy(block, x_buf.at[slot], x_sem.at[slot])

    window = pltpu.make_async_copy(all_ref.at[pl.ds(0, window_ref.shape[0])], window_ref, sems.at[4])

    @pl.when(step == 0)
    def _():
        pairs = ((all_w, w_ref), (all_gain, gain_ref), (all_bias, bias_ref), (all_mask, mask_ref))
        copies = [pltpu.make_async_copy(source, target, sems.at[n]) for n, (source, target) in enumerate(pairs)]
        fetch(0).start()
        for copy in copies:
            copy.start()
        window.start()
        for copy in copies:
            copy.wait()
        gather_weights(w_ref, wt_ref)
        turn_affine(gain_ref, bias_ref, affine_ref)

    @pl.when(step + 1 < steps)
    def _():
        fetch(step + 1).start()

    @pl.when(step + 1 == steps)
    def _():
        window.wait()

    weights = wt_ref[...]
    fetch(step).wait()
    x_ref = x_buf.at[step % 2]
    for k in range(rows):
        proj = jnp.dot(weights, normed_row(x_ref, affine_ref, k), preferred_element_type=f32)
        keep = mask_ref[pl.ds(step * rows + k, 1), :].astype(f32)
        act = (jnp.tanh(proj[: 4 * size]) + 1.0) * proj[4 * size :] * keep
        for lane in range(width // LANES):
            hold[lane, pl.ds(k * stride, 4 * size), :] = act[:, lane * LANES : (lane + 1) * LANES]
    span = pl.ds(pl.multiple_of(step * rows, rows), rows)
    for owner in range(2):
        base = jnp.where(lax.axis_index("row") % 2 == owner, 0, size)
        offset = 0
        for out, count in zip(outs[owner], chunks):
            for side in range(2):
                for h in range(count):
                    for lane in range(width // LANES):
                        start = base + 2 * side * size + offset + h
                        tile = hold[lane, pl.ds(start, rows, stride=stride), :]
                        out[side, h, span, lane * LANES : (lane + 1) * LANES] = tile.astype(bf16)
            offset += count


def project(x, mask, gain, bias, w_proj, chunks, window, vmem, after):
    depth, width, chan = x.shape
    rows, size = PROJECT_ROWS, sum(chunks)
    stride = 4 * size + 4
    return call(
        functools.partial(project_body, chunks, stride),
        (depth // rows,),
        [pl.BlockSpec(memory_space=pltpu.HBM)] * 5,
        [IN_PLACE] * (2 * len(chunks) + 1),
        [pltpu.VMEM((2, size, depth, width), bf16) for size in chunks] * 2 + [pltpu.VMEM((window, width, chan), bf16)],
        [
            pltpu.VMEM((width // LANES, (rows + 1) * stride, LANES), f32),
            pltpu.VMEM((8 * size, chan), bf16),
            pltpu.VMEM((2, chan, LANES), f32),
            pltpu.VMEM((2, rows, width, chan), bf16),
            pltpu.VMEM((depth, width), mask.dtype),
            pltpu.VMEM((1, chan), f32),
            pltpu.VMEM((1, chan), f32),
            pltpu.VMEM(w_proj.shape, bf16),
            pltpu.SemaphoreType.DMA((2,)),
            pltpu.SemaphoreType.DMA((5,)),
        ],
        (2 * depth * width * chan * 8 * size, 4 * depth * width * chan),
        (x, mask, gain.reshape(1, chan), bias.reshape(1, chan), w_proj),
        after,
        vmem,
    )


def gate_body(x_ref, gain_ref, bias_ref, w_ref, out_ref, affine_ref):
    turn_affine(gain_ref, bias_ref, affine_ref)
    weights = w_ref[...]
    for k in range(x_ref.shape[0]):
        normed = normed_row(x_ref, affine_ref, k)
        proj = lax.dot_general(normed, weights, (((0,), (0,)), ((), ())), preferred_element_type=f32)
        out_ref[k] = 0.5 * jnp.tanh(0.5 * proj) + 0.5


def gate(x, gain, bias, w_gate, after):
    rows, width, chan = x.shape
    return call(
        gate_body,
        (1,),
        [IN_PLACE] * 4,
        IN_PLACE,
        pltpu.VMEM(x.shape, f32),
        [pltpu.VMEM((2, chan, LANES), f32)],
        (2 * rows * width * chan * chan, 6 * rows * width * chan),
        (x, gain.reshape(1, chan), bias.reshape(1, chan), w_gate),
        after,
    )


def triangle_body(order, own_ref, got_ref, keep_ref, send_ref, hold):
    count, slots, block, _ = keep_ref.shape
    device = lax.axis_index("row")
    for h in range(count):
        left = jnp.concatenate([own_ref[0, h], got_ref[0, h]], axis=0)
        right = jnp.concatenate([own_ref[1, h], got_ref[1, h]], axis=0)
        hold[h % 4] = lax.dot_general(left, right, (((0,), (0,)), ((), ())), preferred_element_type=f32)
        for slot in range(2 * slots):
            mask = 0
            for digit, bit in enumerate(reversed(order)):
                mask |= (slot >> digit & 1) << bit
            rows = pl.ds(pl.multiple_of((device ^ mask) // 2 * block, block), block)
            if slot < slots:
                keep_ref[h, slot] = hold[h % 4, rows, :]
            else:
                send_ref[h, slot - slots] = hold[h % 4, rows, :].astype(bf16)


def triangle(own, got, order, after):
    _, size, depth, width = own.shape
    slots = 2 ** (len(order) - 1)
    shape = (size, slots, width // (2 * slots), width)
    return call(
        functools.partial(triangle_body, order),
        (1,),
        [IN_PLACE] * 2,
        [IN_PLACE] * 2,
        [pltpu.VMEM(shape, f32), pltpu.VMEM(shape, bf16)],
        [pltpu.VMEM((4, width, width), f32)],
        (4 * size * depth * width * width, 8 * size * depth * width + 3 * size * width * width),
        (own, got),
        after,
    )


def halve_body(held_ref, got_ref, keep_ref, send_ref):
    slots = keep_ref.shape[1]
    keep_ref[...] = held_ref[:, :slots] + got_ref[:, :slots].astype(f32)
    send_ref[...] = (held_ref[:, slots:] + got_ref[:, slots:].astype(f32)).astype(bf16)


def halve(held, got, after):
    count, slots, block, width = held.shape
    shape = (count, slots // 2, block, width)
    return call(
        halve_body,
        (1,),
        [IN_PLACE] * 2,
        [IN_PLACE] * 2,
        [pltpu.VMEM(shape, f32), pltpu.VMEM(shape, bf16)],
        [],
        (held.size, held.size * 9),
        (held, got),
        after,
    )


def total_body(held_ref, got_ref, mine_ref, theirs_ref, hold):
    hold[...] = held_ref[:, 0] + got_ref[:, 0].astype(f32)
    rows = mine_ref.shape[1]
    core = lax.axis_index("row") % 2
    mine_ref[...] = hold[:, pl.ds(pl.multiple_of(core * rows, rows), rows), :]
    theirs_ref[...] = hold[:, pl.ds(pl.multiple_of((1 - core) * rows, rows), rows), :]


def total(held, got, after):
    count, _, block, width = held.shape
    shape = pltpu.VMEM((count, block // 2, width), f32)
    return call(
        total_body,
        (1,),
        [IN_PLACE] * 2,
        [IN_PLACE] * 2,
        [shape, shape],
        [pltpu.VMEM((count, block, width), f32)],
        (held.size, held.size * 10),
        (held, got),
        after,
    )


def finish_body(chunks, *refs):
    count = len(chunks)
    parts = refs[:count], refs[count : 2 * count]
    gate_ref, gain_ref, bias_ref, w_ref, all_ref, hold, wide_ref, out_ref, sems = refs[2 * count :]
    hidden, chan = w_ref.shape
    half = hidden // 2
    rows, width, _ = gate_ref.shape
    stride = hold.shape[1] // hidden

    values = [part[h] for side in parts for part in side for h in range(part.shape[0])]
    mean_val = sum(values) * (1.0 / hidden)
    square = sum((value - mean_val) * (value - mean_val) for value in values)
    scale = lax.rsqrt(square * (1.0 / hidden) + EPS)
    base = lax.axis_index("row") % 2 * half
    for place, value in enumerate(values):
        index = base + place if place < half else place - base
        value = (value - mean_val) * scale * gain_ref[index] + bias_ref[index]
        for lane in range(width // LANES):
            hold[lane, place * stride : place * stride + rows, :] = value[:, lane * LANES : (lane + 1) * LANES]
    wide_ref[...] = jnp.zeros_like(wide_ref)
    for place, start in ((0, base), (half, half - base)):
        block = w_ref[pl.ds(pl.multiple_of(start, half), half), :]
        wide_ref[place : place + half, :chan] = block
        wide_ref[hidden + place : hidden + place + half, chan:] = block

    weights = wide_ref[...]
    copies = []
    for row in range(0, rows, 2):
        for lane in range(width // LANES):
            pair = [hold[lane, pl.ds(row + n, hidden, stride=stride), :].astype(bf16) for n in range(2)]
            normed = jnp.concatenate(pair, axis=0)
            mixed = lax.dot_general(normed, weights, (((0,), (0,)), ((), ())), preferred_element_type=f32)
            span = pl.ds(lane * LANES, LANES)
            for n in range(2):
                value = gate_ref[row + n, span, :] * mixed[:, n * chan : (n + 1) * chan]
                out_ref[row + n, span, :] = value.astype(bf16)
        if row % 4 == 2:
            block = pl.ds(row - 2, 4)
            copies.append(pltpu.make_async_copy(out_ref.at[block], all_ref.at[block], sems.at[row // 4]))
            copies[-1].start()
    for copy in copies:
        copy.wait()


def finish(mine, theirs, gate_act, gain, bias, w_out, chunks):
    rows, width, chan = gate_act.shape
    hidden = w_out.shape[0]
    stride = rows + 8
    smem = pl.BlockSpec(memory_space=pltpu.SMEM)
    return call(
        functools.partial(finish_body, chunks),
        (1,),
        [IN_PLACE] * (2 * len(mine) + 1) + [smem, smem, IN_PLACE],
        pl.BlockSpec(memory_space=pltpu.HBM),
        jax.ShapeDtypeStruct((rows, width, chan), bf16),
        [
            pltpu.VMEM((width // LANES, (hidden + 1) * stride, LANES), f32),
            pltpu.VMEM((2 * hidden, 2 * chan), bf16),
            pltpu.VMEM((rows, width, chan), bf16),
            pltpu.SemaphoreType.DMA((rows // 4,)),
        ],
        (2 * rows * width * chan * hidden, rows * width * (chan * 6 + hidden * 4)),
        (*mine, *theirs, gate_act, gain, bias, w_out),
    )


def in_turn(orders):
    events, turn = [], 0
    for chunk, order in enumerate(orders):
        late = order[0] != 1
        for step in range(len(order) + 1):
            if late:
                time = step + 2 * (step == len(order))
            else:
                time = turn + step if step else max(turn - 1, 0)
            events.append((time, step == 0, late and step > 0, step, chunk))
        turn += not late
    return [(chunk, step) for *_, step, chunk in sorted(events)]


def on_device(pair_act, pair_mask, in_gain, in_bias, w_proj, w_gate, out_gain, out_bias, w_out):
    width = pair_act.shape[1]
    devices = lax.axis_size("row")
    bits = devices.bit_length() - 1
    unit = w_out.shape[0] // 32
    z_last, z_first = tuple(range(1, bits)), tuple(range(2, bits)) + (1,)
    plan = ((4, z_last), (3, z_first), (4, z_last), (3, z_last), (2, z_last))
    chunks, orders = tuple(size * unit for size, _ in plan), tuple(order for _, order in plan)
    count = len(chunks)

    def swap(values, bit):
        return lax.ppermute(values, "row", [(d, d ^ 1 << bit) for d in range(devices)])

    last = []

    def put(kernel, *operands):
        outs = kernel(*operands, tuple(last[-1:]))
        last.append(outs[0] if isinstance(outs, (list, tuple)) else outs)
        return outs

    vmem = (61 << 20) - pair_act.shape[0] * width * w_out.shape[0] * 4
    acts = put(
        project, pair_act, pair_mask, in_gain, in_bias, w_proj, chunks, width // devices, vmem
    )
    own, got = acts[:count], [swap(part, 0) for part in acts[count:-1]]
    held, arrived = {}, {}

    def advance(chunk, step):
        order = orders[chunk]
        if step == 0:
            held[chunk], sent = put(triangle, own[chunk], got[chunk], order)
        elif step < len(order):
            held[chunk], sent = put(halve, held[chunk], arrived[chunk])
        else:
            held[chunk], sent = put(total, held[chunk], arrived[chunk])
        arrived[chunk] = swap(sent, order[step] if step < len(order) else 0)

    sequence = in_turn(orders)
    for position, (chunk, step) in enumerate(sequence):
        with jax.named_scope(f"chunk{chunk}_step{step}"):
            advance(chunk, step)
        if position == 1:
            gate_act = put(gate, acts[-1], in_gain, in_bias, w_gate)
    mine, theirs = [held[c] for c in range(count)], [arrived[c] for c in range(count)]
    return finish(mine, theirs, gate_act, out_gain, out_bias, w_out, chunks)


def solution(mesh):
    return jax.shard_map(
        on_device,
        mesh=mesh,
        in_specs=(
            P(("groups", "row"), None, None),
            P(("groups", "row"), None),
            P(),
            P(),
            P(),
            P(),
            P(),
            P(),
            P(),
        ),
        out_specs=P(("groups", "row"), None, None),
        check_vma=False,
    )
```
